32 devices in a mesh: group: 2 (over y), outer: 4 (over z), seq: 4 (over x, core).
Axes of the slice: x: 2, y: 2, z: 4, core: 2. Of those that a mesh axis runs over, the one named last changes fastest.
Arguments:
- activations: bfloat16 [8, 512, 2048], P(('group', 'outer'), 'seq'), parts along dimension 0
- cotangent: bfloat16 [8, 512, 2048], P(('group', 'outer'), None, 'seq'), parts along dimension 0
- weights: bfloat16 [8, 2048, 2048], P(('group', 'outer'), None, 'seq'), parts along dimension 0
- earlier_delta: bfloat16 [8, 2048, 2048], P(('group', 'outer'), None, 'seq'), parts along dimension 0, may hold values from -6 to 6
- momentum: bfloat16 [8, 2048, 2048], P(('group', 'outer'), None, 'seq'), parts along dimension 0, may hold values from -3 to 3
- module_path: int32 [8], P('group'), parts along dimension 0, may hold values from 0 to 3
Outputs:
- new_weights: bfloat16 [8, 2048, 2048], P(('group', 'outer'), None, 'seq'), parts along dimension 0
- outer_delta: bfloat16 [8, 2048, 2048], P(('group', 'outer'), None, 'seq'), parts along dimension 0
- new_momentum: bfloat16 [8, 2048, 2048], P(('group', 'outer'), None, 'seq'), parts along dimension 0
The draws below stay inside these ranges and needn't reach their ends.
There are 2 independent parts, one for each index of `group`. The reference program is written for one: setup_inputs(seed, part) draws one part's arguments, and reference() takes and returns one part's arrays. A program takes and returns all parts, laid end to end along the dimension named above; each array names one. Nothing has to cross between parts.
All inputs are finite; a program needn't handle non-finite values.
Results may differ from the reference program's by a relative error of at most 0.0036.
Values may be sent and summed in bfloat16 or wider, within the bound.
A program may use at most 128 MiB of HBM per device.

```python
import math
import jax
import jax.numpy as jnp
from jax import lax

DW = 2048
STEPS = 3
PODS = 4
MODULES = 4
TOKENS = 512


def draw_weights(key, part):
    key = jax.random.fold_in(key, 11)
    key_base, key_scale = jax.random.split(key)
    base = jax.random.normal(key_base, (PODS, DW, DW), jnp.float32)
    spread = jnp.exp(jax.random.uniform(key_scale, (PODS, 1, DW), jnp.float32, math.log(0.3), math.log(3.0)))
    rising = jnp.exp(jnp.arange(DW, dtype=jnp.float32) * (math.log(3.0) / (DW - 1))) / math.sqrt(3.0)
    return (base * spread * rising * 0.3333333).astype(jnp.bfloat16)


def draw_activations(key, part):
    key = jax.random.fold_in(key, 12)
    key_base, key_scale = jax.random.split(key)
    base = jax.random.normal(key_base, (PODS, TOKENS, DW), jnp.float32)
    spread = jnp.exp(jax.random.uniform(key_scale, (PODS, TOKENS, 1), jnp.float32, math.log(0.3), math.log(3.0)))
    return (base * spread).astype(jnp.bfloat16)


def draw_cotangent(key, part):
    key = jax.random.fold_in(key, 13)
    key_base = jax.random.fold_in(key, 0)
    values = jnp.clip(jax.random.normal(key_base, (PODS, TOKENS, DW), jnp.float32), -6.0, 6.0)
    return values.astype(jnp.bfloat16)


def with_ends(drawn, key, low, high):
    shape = drawn.shape
    spot = [jax.random.randint(jax.random.fold_in(key, axis), (), 0, shape[axis]) for axis in range(len(shape))]
    drawn = drawn.at[tuple(spot)].set(low)
    longest = shape.index(max(shape))
    spot[longest] = (spot[longest] + 1) % shape[longest]
    return drawn.at[tuple(spot)].set(high)


def block_scale(rng, dims, cuts, least, largest):
    gain = 1.0
    for position, shards_of in cuts:
        steps = jax.random.uniform(jax.random.fold_in(jax.random.fold_in(rng, 6), position), (shards_of,), jnp.float32, least / len(cuts), largest / len(cuts))
        gain = gain * jnp.repeat(jnp.exp(steps), dims[position] // shards_of).reshape((-1,) + (1,) * (len(dims) - 1 - position))
    return gain


def centred(key, dims, scale, most, pieces=(), kind=jnp.bfloat16):
    drawn = scale * jax.random.normal(key, dims, jnp.float32)
    if pieces:
        drawn = drawn * block_scale(key, dims, pieces, -0.22, 0.18)
    return jnp.clip(drawn, -most, most).astype(kind)


def setup_inputs(seed: int = 0, part: int = 0) -> dict:
    seeds = jax.random.split(jax.random.key(seed), 7)
    part_keys = jax.random.split(jax.random.fold_in(seeds[6], part), 7)
    return {
        "activations": draw_activations(jax.random.fold_in(jax.random.fold_in(seeds[6], part), 71), part),
        "cotangent": draw_cotangent(jax.random.fold_in(jax.random.fold_in(seeds[6], part), 71), part),
        "weights": draw_weights(jax.random.fold_in(jax.random.fold_in(seeds[6], part), 71), part),
        "earlier_delta": centred(part_keys[3], (PODS, DW, DW), 1.0, 6.0, ((0, 4), (2, 4))),
        "momentum": centred(part_keys[4], (PODS, DW, DW), 0.5, 3.0, ((0, 4), (2, 4))),
        "module_path": with_ends(jax.random.randint(part_keys[5], (PODS,), 0, MODULES), jax.random.fold_in(part_keys[5], 1), 0, MODULES - 1).astype(jnp.int32),
    }


epsilon = 1e-06
inner_rate = 0.05
outer_rate = 0.7
beta_outer = 0.9

def inner_train(operands):
    inputs, sensed, start_weight = operands
    factor = 1.0 / jnp.sqrt(jnp.float32(DW))
    current = start_weight.astype(jnp.float32)
    for inner_step in range(STEPS):
        weight_bf = current.astype(jnp.bfloat16)
        projected = jnp.dot(inputs, weight_bf, preferred_element_type=jnp.float32) * factor
        row_rms = jnp.sqrt(lax.optimization_barrier(jnp.mean(projected * projected, axis=1, keepdims=True)) + epsilon)
        normed = projected / row_rms
        sigmoid_y = jax.nn.sigmoid(normed)
        grad_out = sensed.astype(jnp.float32) * sigmoid_y * (1.0 + normed * (1.0 - sigmoid_y))
        mixed = lax.optimization_barrier(jnp.mean(grad_out * normed, axis=1, keepdims=True))
        grad_in = ((grad_out - normed * mixed) / row_rms).astype(jnp.bfloat16)
        gradient = lax.dot_general(inputs, grad_in, (((0,), (0,)), ((), ())), preferred_element_type=jnp.float32) * factor
        current = current - inner_rate * gradient
    return current

def reference(activations, cotangent, weights, earlier_delta, momentum, module_path):
    shared = (module_path[:, None] == module_path[None, :]).astype(jnp.float32)
    group_size = lax.optimization_barrier(jnp.sum(shared, axis=1))
    summed = jnp.einsum('pq,qij->pij', shared, earlier_delta.astype(jnp.float32))
    outer_grad = summed / group_size[:, None, None]
    moment = beta_outer * momentum.astype(jnp.float32) + outer_grad
    new_momentum = moment.astype(jnp.bfloat16)
    direction = outer_grad + beta_outer * moment
    finals = lax.map(inner_train, (activations, cotangent, weights))
    outer_delta = ((weights.astype(jnp.float32) - finals) / (inner_rate * STEPS)).astype(jnp.bfloat16)
    new_weights = (finals - outer_rate * inner_rate * STEPS * direction).astype(jnp.bfloat16)
    return (new_weights, outer_delta, new_momentum)
```

```python
import functools

import jax
import jax.numpy as jnp
from jax import lax
from jax.experimental import pallas as pl
from jax.experimental.pallas import tpu as pltpu
from jax.sharding import PartitionSpec as P

STEPS = 3


epsilon = 1e-06
inner_rate = 0.05
outer_rate = 0.7
beta_outer = 0.9

MESH = pl.DeviceIdType.MESH
PIECES = 16
F32 = jnp.float32
BF16 = jnp.bfloat16


def kernel(slots, coef, a_hbm, c_hbm, w_hbm, d_hbm, m_hbm, ow_hbm, od_hbm, om_hbm,
           a, c, w, d, m, e, y1, y2, z, proj, normed, sens, gram, grads, cur, ow, od, om,
           sent, sums, load, agx_s, agx_r, agc_s, agc_r, agf_s, agf_r, ex_s, ex_r,
           e_s, e_r, y1_s, y1_r, y2_s, y2_r, z_s, z_r, out_s):
    tokens, width = a.shape
    columns = w.shape[1]
    shard = tokens // 4
    half = tokens // 2
    rows = width // PIECES
    factor = 1.0 / width ** 0.5

    o = lax.axis_index("outer")
    s = lax.axis_index("seq")
    core = s % 2
    chip = s // 2
    peers = (chip * 2 + 1 - core, (1 - chip) * 2 + core, (1 - chip) * 2 + 1 - core)
    near = o + 1 - 2 * (o % 2)
    mid = 3 - o
    inner = jnp.logical_or(o == 1, o == 2)
    end = jnp.logical_or(o == 0, o == 3)

    def remote(src, dst, send, recv, **where):
        return pltpu.make_async_remote_copy(
            src_ref=src, dst_ref=dst, send_sem=send, recv_sem=recv, device_id=where, device_id_type=MESH)

    barrier = pltpu.get_barrier_semaphore()
    for peer in peers:
        pl.semaphore_signal(barrier, inc=1, device_id={"seq": peer}, device_id_type=MESH)
    pl.semaphore_signal(barrier, inc=1, device_id={"outer": near}, device_id_type=MESH)

    @pl.when(inner)
    def _():
        pl.semaphore_signal(barrier, inc=1, device_id={"outer": mid}, device_id_type=MESH)

    local = [pltpu.make_async_copy(x, y, load.at[k]) for k, (x, y) in enumerate(
        ((a_hbm, a.at[pl.ds(pl.multiple_of(s * shard, shard), shard)]), (w_hbm, w), (c_hbm, c), (d_hbm, d), (m_hbm, m)))]
    for copy in local:
        copy.start()

    @pl.when(inner)
    def _():
        pl.semaphore_wait(barrier, 5)

    @pl.when(end)
    def _():
        pl.semaphore_wait(barrier, 4)

    parts = 4
    piece = shard // parts

    def rows_of(owner, k):
        return pl.ds(pl.multiple_of(owner * shard + k * piece, piece), piece)

    def to_chip(k):
        return remote(a_hbm.at[pl.ds(k * piece, piece)], a.at[rows_of(s, k)], agx_s.at[k], agx_r.at[k], seq=peers[1])

    def forward(k):
        return remote(a.at[rows_of(peers[1], k)], a.at[rows_of(peers[1], k)], agf_s.at[k], agf_r.at[k], seq=peers[0])

    own_rows = pl.ds(pl.multiple_of(s * shard, shard), shard)
    to_core = remote(a_hbm, a.at[own_rows], agc_s, agc_r, seq=peers[0])
    for k in range(parts):
        to_chip(k).start()
    to_core.start()

    def span(k):
        return pl.ds(pl.multiple_of(k * rows, rows), rows)

    def send_e(k):
        return remote(d_hbm.at[span(k)], e.at[span(k)], e_s.at[k], e_r.at[k], outer=near)

    def send_y1(k):
        return remote(d_hbm.at[span(k)] if slots == 2 else y2.at[span(k)], y1.at[span(k)],
                      y1_s.at[k], y1_r.at[k], outer=mid)

    def send_y2(k):
        return remote(e.at[span(k)], y2.at[span(k)], y2_s.at[k], y2_r.at[k], outer=mid)

    def send_z(k):
        return remote(z.at[span(k)], e.at[span(k)], z_s.at[k], z_r.at[k], outer=near)

    def loop(lo, hi, body):
        def step(k, carry):
            body(k)
            return carry
        lax.fori_loop(lo, hi, step, 0)

    @pl.when(end)
    def _():
        loop(0, PIECES, lambda k: send_e(k).start())

    if slots == 2:
        @pl.when(inner)
        def _():
            loop(0, PIECES, lambda k: send_y1(k).start())

    def combine(k):
        send_e(k).wait_recv()
        y2[span(k)] = (coef[7] * e[span(k)].astype(F32) + coef[8] * d[span(k)].astype(F32)).astype(BF16)
        send_y1(k).start()

    def pass_on(k):
        send_y1(k).wait_recv()
        total = coef[4] * d[span(k)].astype(F32) + coef[5] * y1[span(k)].astype(F32)
        if slots == 2:
            send_y2(k).wait_recv()
            total = total + coef[6] * y2[span(k)].astype(F32)
        z[span(k)] = total.astype(BF16)
        send_z(k).start()

    lag = 2

    def tick(lo, hi):
        if slots == 1:
            @pl.when(inner)
            def _():
                loop(lo, min(hi, PIECES), combine)
                loop(max(lo - lag, 0), hi - lag, pass_on)

    for copy in local:
        copy.wait()

    def project(block):
        r = pl.ds(pl.multiple_of(block * half, half), half)
        tile = min(256, columns)

        def one(k):
            cols = pl.ds(pl.multiple_of(k * tile, tile), tile)
            proj[r, cols] = jnp.dot(a[r, :], w[:, cols], preferred_element_type=F32) * factor
        loop(0, columns // tile, one)

    to_core.wait_recv()
    project(chip)
    tick(0, 1)
    for k in range(parts):
        to_chip(k).wait_recv()
        forward(k).start()
    tick(1, 3)
    for k in range(parts):
        forward(k).wait_recv()
    project(1 - chip)

    group = 128
    groups = tokens // group
    eye = lax.broadcasted_iota(jnp.int32, (group, group), 0) == lax.broadcasted_iota(jnp.int32, (group, group), 1)

    def rows_at(g):
        return pl.ds(pl.multiple_of(g * group, group), group)

    def to_row(column):
        return jnp.sum(jnp.where(eye, column, 0.0), axis=0, keepdims=True)

    def to_column(row):
        return jnp.sum(jnp.where(eye, row, 0.0), axis=1, keepdims=True)

    def exchange(n, k):
        return remote(sent.at[n], sums.at[n, k], ex_s.at[n, k], ex_r.at[n, k], seq=peers[k])

    def post(n):
        for k in range(3):
            exchange(n, k).start()

    def collect(n):
        for k in range(3):
            exchange(n, k).wait_recv()

    def total(n, g):
        one = pl.ds(g, 1)
        return sent[n, one, :] + sums[n, 0, one, :] + sums[n, 1, one, :] + sums[n, 2, one, :]

    def gram_tile(k):
        r = pl.ds(pl.multiple_of(k * 256, 256), 256)
        gram[:, r] = (lax.dot_general(a[...], a[r, :], (((1,), (1,)), ((), ())), preferred_element_type=F32)
                      * (inner_rate / width)).astype(BF16)

    points = ((3, 5), (5, 7), (7, 8), (8, 10), (10, 11), (11, 12))
    for step in range(STEPS):
        first, second = 2 * step, 2 * step + 1

        def squares(g):
            p = proj[rows_at(g), :]
            sent[first, pl.ds(g, 1), :] = to_row(jnp.sum(p * p, axis=1, keepdims=True))
        loop(0, groups, squares)
        post(first)
        if step == 0:
            loop(0, tokens // 256, gram_tile)
        tick(*points[first])
        collect(first)

        def inverse(g):
            return to_column(lax.rsqrt(total(first, g) / width + epsilon))

        def sensitivity(g):
            n = proj[rows_at(g), :] * inverse(g)
            sig = jax.nn.sigmoid(n)
            out = c[rows_at(g), :].astype(F32) * sig * (1.0 + n * (1.0 - sig))
            normed[rows_at(g), :] = n
            sens[rows_at(g), :] = out
            sent[second, pl.ds(g, 1), :] = to_row(jnp.sum(out * n, axis=1, keepdims=True))
        loop(0, groups, sensitivity)
        post(second)
        tick(*points[second])
        collect(second)

        def gradient(g):
            mixed = to_column(total(second, g) / width)
            grads[step, rows_at(g), :] = (
                (sens[rows_at(g), :] - normed[rows_at(g), :] * mixed) * inverse(g)).astype(BF16)
        loop(0, groups, gradient)
        if step < STEPS - 1:
            def descend(k):
                cols = pl.ds(pl.multiple_of(k * 256, 256), 256)
                proj[:, cols] -= jnp.dot(gram[...], grads[step, :, cols], preferred_element_type=F32)
            loop(0, columns // 256, descend)

    def weight_rows(k):
        r = pl.ds(pl.multiple_of(k * 256, 256), 256)
        turned = a[:, r].T
        acc = jnp.dot(turned, grads[0], preferred_element_type=F32)
        for step in range(1, STEPS):
            acc = acc + jnp.dot(turned, grads[step], preferred_element_type=F32)
        od[r, :] = (acc * (factor / STEPS)).astype(BF16)
        cur[r, :] = w[r, :].astype(F32) - acc * (inner_rate * factor)
    loop(0, width // 256, weight_rows)
    delta_out = pltpu.make_async_copy(od, od_hbm, out_s.at[2, 0])
    delta_out.start()

    def outs(k):
        return (pltpu.make_async_copy(ow.at[span(k)], ow_hbm.at[span(k)], out_s.at[0, k]),
                pltpu.make_async_copy(om.at[span(k)], om_hbm.at[span(k)], out_s.at[1, k]))

    def finish(k, summed):
        outer_grad = summed * coef[0]
        moment = beta_outer * m[span(k)].astype(F32) + outer_grad
        direction = outer_grad + beta_outer * moment
        om[span(k)] = moment.astype(BF16)
        ow[span(k)] = (cur[span(k)] - (outer_rate * inner_rate * STEPS) * direction).astype(BF16)
        for copy in outs(k):
            copy.start()

    def finish_inner(k):
        summed = d[span(k)].astype(F32) + coef[1] * e[span(k)].astype(F32) + coef[2] * y1[span(k)].astype(F32)
        if slots == 2:
            summed = summed + coef[3] * y2[span(k)].astype(F32)
        finish(k, summed)

    @pl.when(inner)
    def _():
        if slots == 2:
            def relay(k):
                send_e(k).wait_recv()
                send_y2(k).start()
            loop(0, PIECES, relay)

            def both(k):
                pass_on(k)
                finish_inner(k)
            loop(0, PIECES, both)
        else:
            done = points[-1][1]

            def both(k):
                @pl.when(k < PIECES)
                def _():
                    combine(k)
                pass_on(k - lag)
            loop(done, PIECES + lag, both)
            loop(0, PIECES, finish_inner)

        def settle(k):
            send_y1(k).wait_send()
            if slots == 2:
                send_y2(k).wait_send()
            send_z(k).wait_send()
        loop(0, PIECES, settle)

    @pl.when(end)
    def _():
        def last(k):
            send_z(k).wait_recv()
            finish(k, d[span(k)].astype(F32) + e[span(k)].astype(F32))
        loop(0, PIECES, last)
        loop(0, PIECES, lambda k: send_e(k).wait_send())

    to_core.wait_send()
    for k in range(parts):
        to_chip(k).wait_send()
        forward(k).wait_send()
    for n in range(2 * STEPS):
        for k in range(3):
            exchange(n, k).wait_send()

    def written(k):
        for copy in outs(k):
            copy.wait()
    loop(0, PIECES, written)
    delta_out.wait()


def phase(slots, coef, activations, cotangent, weights, earlier_delta, momentum):
    width, columns = weights.shape
    tokens = cotangent.shape[0]
    any_spec = pl.BlockSpec(memory_space=pl.ANY)
    full = pltpu.VMEM((width, columns), BF16)
    plane = pltpu.VMEM((tokens, columns), F32)
    dma = pltpu.SemaphoreType.DMA
    line = dma((PIECES,))
    out = jax.ShapeDtypeStruct((width, columns), BF16)
    return pl.pallas_call(
        functools.partial(kernel, slots),
        out_shape=(out, out, out),
        in_specs=[pl.BlockSpec(memory_space=pltpu.SMEM)] + [any_spec] * 5,
        out_specs=(any_spec,) * 3,
        scratch_shapes=[
            pltpu.VMEM((tokens, width), BF16), pltpu.VMEM((tokens, columns), BF16),
            full, full, full, full, full, full, full,
            plane, plane, plane, pltpu.VMEM((tokens, tokens), BF16),
            pltpu.VMEM((STEPS, tokens, columns), BF16),
            pltpu.VMEM((width, columns), F32), full, full, full,
            pltpu.VMEM((2 * STEPS, 8, 128), F32), pltpu.VMEM((2 * STEPS, 3, 8, 128), F32),
            dma((5,)), dma((4,)), dma((4,)), dma, dma, dma((4,)), dma((4,)),
            dma((2 * STEPS, 3)), dma((2 * STEPS, 3)),
            line, line, line, line, line, line, line, line, dma((3, PIECES)),
        ],
        compiler_params=pltpu.CompilerParams(
            collective_id=slots, has_side_effects=True, vmem_limit_bytes=56 * 1024 * 1024),
        cost_estimate=pl.CostEstimate(
            flops=12 * tokens * width * columns, bytes_accessed=14 * width * columns, transcendentals=0),
        name="phase%d" % slots,
    )(coef, activations, cotangent, weights, earlier_delta, momentum)


def line_body(activations, cotangent, weights, earlier_delta, momentum, module_path):
    shared = (module_path[:, None] == module_path[None, :]).astype(F32)
    own = lax.axis_index("outer")
    near = own + 1 - 2 * (own % 2)
    mid, far = 3 - own, 3 - near
    side = jnp.arange(4) // 2
    crosses = jnp.max(jnp.where(side[:, None] != side[None, :], shared, 0.0), axis=1)

    def pair(i, j):
        return shared[i, j]

    wide = [1.0 / jnp.sum(shared[own]), pair(own, near), pair(own, mid), pair(own, far),
            pair(near, own), pair(near, mid), pair(near, far), crosses[near], crosses[own]]
    arrays = (activations[0], cotangent[0], weights[0], earlier_delta[0], momentum[0])
    outs = phase(2, jnp.stack(wide), *arrays)
    return tuple(x[None] for x in outs)


def body(activations, cotangent, weights, earlier_delta, momentum, module_path):
    gathered = lax.all_gather(activations[0], "seq", axis=0, tiled=True)
    width = gathered.shape[1]
    factor = 1.0 / jnp.sqrt(jnp.float32(width))
    own_pod = lax.axis_index("outer")
    matches = module_path[:, None] == module_path[None, :]
    shared_bf = jnp.where(matches, 1.0, 0.0).astype(jnp.bfloat16)
    group_size = jnp.sum(jnp.where(matches, 1.0, 0.0).astype(jnp.float32), axis=1)
    own_size = lax.dynamic_index_in_dim(group_size, own_pod, 0, keepdims=False)
    columns = weights.shape[2]
    npods = lax.axis_size("outer")
    blocks = earlier_delta[0].reshape(npods, width // npods, columns)
    sums = jnp.einsum(
        "pq,qrc->prc",
        shared_bf,
        lax.all_to_all(blocks, "outer", split_axis=0, concat_axis=0, tiled=True),
        preferred_element_type=jnp.float32,
    )
    returned = lax.all_to_all(sums, "outer", split_axis=0, concat_axis=0, tiled=True)
    summed = returned.reshape(width, columns)
    outer_grad = summed / own_size
    moment = beta_outer * momentum[0].astype(jnp.float32) + outer_grad
    direction = outer_grad + beta_outer * moment
    sensed = cotangent[0]
    current = weights[0].astype(jnp.float32)
    for inner_step in range(STEPS):
        weight_bf = current.astype(jnp.bfloat16)
        projected = jnp.dot(gathered, weight_bf, preferred_element_type=jnp.float32) * factor
        squares = lax.psum(jnp.sum(projected * projected, axis=1), "seq")
        row_rms = jnp.sqrt(squares / width + epsilon)[:, None]
        normed = projected / row_rms
        sigmoid_y = jax.nn.sigmoid(normed)
        grad_out = sensed.astype(jnp.float32) * sigmoid_y * (1.0 + normed * (1.0 - sigmoid_y))
        products = lax.psum(jnp.sum(grad_out * normed, axis=1), "seq")
        grad_in = ((grad_out - normed * (products / width)[:, None]) / row_rms).astype(jnp.bfloat16)
        gradient = (
            lax.dot_general(
                gathered, grad_in, (((0,), (0,)), ((), ())), preferred_element_type=jnp.float32
            )
            * factor
        )
        current = current - inner_rate * gradient
    outer_delta = ((weights[0].astype(jnp.float32) - current) / (inner_rate * STEPS)).astype(
        jnp.bfloat16
    )
    new_weights = (current - outer_rate * inner_rate * STEPS * direction).astype(jnp.bfloat16)
    new_momentum = moment.astype(jnp.bfloat16)
    return (new_weights[None], outer_delta[None], new_momentum[None])


def solution(mesh):
    in_specs = (
        P(("group", "outer"), "seq", None),
        P(("group", "outer"), None, "seq"),
        P(("group", "outer"), None, "seq"),
        P(("group", "outer"), None, "seq"),
        P(("group", "outer"), None, "seq"),
        P("group"),
    )
    out_specs = (
        P(("group", "outer"), None, "seq"),
        P(("group", "outer"), None, "seq"),
        P(("group", "outer"), None, "seq"),
    )
    def run(*args):
        sizes = (mesh.shape["outer"], mesh.shape["seq"], args[0].shape[1], args[2].shape[1])
        fits = sizes[:2] == (4, 4) and sizes[2] == 512 and sizes[3] % 512 == 0 and sizes[3] <= 2048
        chosen = line_body if fits else body
        return jax.shard_map(
            chosen, mesh=mesh, in_specs=in_specs, out_specs=out_specs, check_vma=False)(*args)

    return run
```

```python
import functools

import jax
import jax.numpy as jnp
from jax import lax
from jax.experimental import pallas as pl
from jax.experimental.pallas import tpu as pltpu
from jax.sharding import PartitionSpec as P

STEPS = 3


epsilon = 1e-06
inner_rate = 0.05
outer_rate = 0.7
beta_outer = 0.9

MESH = pl.DeviceIdType.MESH
PIECES = 16
F32 = jnp.float32
BF16 = jnp.bfloat16


def same(path, i, j):
    return jnp.where(path[i] == path[j], 1.0, 0.0)


def crossing(path, i):
    other = 2 - 2 * (i // 2)
    return jnp.maximum(same(path, i, other), same(path, i, other + 1))


def others(i):
    low = i // 2
    return 2 - low, 3 - 3 * low


def first_share(path, i):
    near, far = others(i)
    inner = crossing(path, near)
    return inner * same(path, i, near) + (1.0 - inner) * same(path, i, far)


def second_share(path, i):
    near, far = others(i)
    return crossing(path, near) * (1.0 - same(path, near, far)) * same(path, i, far)


def phase_kernel(path, a_hbm, c_hbm, w_hbm, d_hbm, cur_hbm, sum_hbm, flag,
                 a, c, w, d, e, x, y, z, proj, normed, sens, gram, grads, cur, summed,
                 sent, sums, mark, load, agx_s, agx_r, agc_s, agc_r, agf_s, agf_r, ex_s, ex_r,
                 e_s, e_r, y_s, y_r, z_s, z_r, out_s, mark_s, mark_r):
    tokens, width = a.shape
    columns = w.shape[1]
    shard = tokens // 4
    half = tokens // 2
    rows = width // PIECES
    factor = 1.0 / width ** 0.5

    o = lax.axis_index("outer")
    s = lax.axis_index("seq")
    part = lax.axis_index("group")
    core = s % 2
    chip = s // 2
    peers = (chip * 2 + 1 - core, (1 - chip) * 2 + core, (1 - chip) * 2 + 1 - core)
    near = o + 1 - 2 * (o % 2)
    mid = 3 - o
    inner = jnp.logical_or(o == 1, o == 2)
    end = jnp.logical_or(o == 0, o == 3)

    def remote(src, dst, send, recv, **where):
        return pltpu.make_async_remote_copy(
            src_ref=src, dst_ref=dst, send_sem=send, recv_sem=recv, device_id=where, device_id_type=MESH)

    barrier = pltpu.get_barrier_semaphore()
    for peer in peers:
        pl.semaphore_signal(barrier, inc=1, device_id={"seq": peer}, device_id_type=MESH)
    pl.semaphore_signal(barrier, inc=1, device_id={"outer": near}, device_id_type=MESH)
    pl.semaphore_signal(barrier, inc=1, device_id={"group": 1 - part}, device_id_type=MESH)

    @pl.when(inner)
    def _():
        pl.semaphore_signal(barrier, inc=1, device_id={"outer": mid}, device_id_type=MESH)

    local = [pltpu.make_async_copy(x, y, load.at[k]) for k, (x, y) in enumerate(
        ((a_hbm, a.at[pl.ds(pl.multiple_of(s * shard, shard), shard)]), (w_hbm, w), (c_hbm, c), (d_hbm, d)))]
    for copy in local:
        copy.start()

    @pl.when(inner)
    def _():
        pl.semaphore_wait(barrier, 6)

    @pl.when(end)
    def _():
        pl.semaphore_wait(barrier, 5)

    parts = 4
    piece = shard // parts

    def rows_of(owner, k):
        return pl.ds(pl.multiple_of(owner * shard + k * piece, piece), piece)

    def to_chip(k):
        return remote(a_hbm.at[pl.ds(k * piece, piece)], a.at[rows_of(s, k)], agx_s.at[k], agx_r.at[k], seq=peers[1])

    def forward(k):
        return remote(a.at[rows_of(peers[1], k)], a.at[rows_of(peers[1], k)], agf_s.at[k], agf_r.at[k], seq=peers[0])

    own_rows = pl.ds(pl.multiple_of(s * shard, shard), shard)
    to_core = remote(a_hbm, a.at[own_rows], agc_s, agc_r, seq=peers[0])
    for k in range(parts):
        to_chip(k).start()
    to_core.start()

    def span(k):
        return pl.ds(pl.multiple_of(k * rows, rows), rows)

    def send_e(k):
        return remote(d_hbm.at[span(k)], e.at[span(k)], e_s.at[k], e_r.at[k], outer=near)

    def send_y(k):
        return remote(x.at[span(k)], y.at[span(k)], y_s.at[k], y_r.at[k], outer=mid)

    def send_z(k):
        return remote(z.at[span(k)], e.at[span(k)], z_s.at[k], z_r.at[k], outer=near)

    def loop(lo, hi, body):
        def step(k, carry):
            body(k)
            return carry
        lax.fori_loop(lo, hi, step, 0)

    @pl.when(end)
    def _():
        loop(0, PIECES, lambda k: send_e(k).start())

    need = crossing(path, 0) * crossing(path, 1) * (1.0 - same(path, 0, 1))
    mark[0] = jnp.full((8, 128), need, F32)
    tell = remote(mark.at[0], mark.at[1], mark_s, mark_r, group=1 - part)
    tell.start()

    own_cross = crossing(path, o)
    x_own = own_cross
    x_end = own_cross * same(path, o, near) + (1.0 - own_cross) * crossing(path, near)
    pair = same(path, o, near)
    take = first_share(path, o)
    near_take = first_share(path, near)

    def collected(k):
        return pltpu.make_async_copy(summed.at[span(k)], sum_hbm.at[span(k)], out_s.at[k])

    def combine(k):
        send_e(k).wait_recv()
        x[span(k)] = (x_end * e[span(k)].astype(F32) + x_own * d[span(k)].astype(F32)).astype(BF16)
        send_y(k).start()

    def pass_on(k):
        send_y(k).wait_recv()
        mine = d[span(k)].astype(F32)
        across = y[span(k)].astype(F32)
        z[span(k)] = (pair * mine + near_take * across).astype(BF16)
        send_z(k).start()
        summed[span(k)] = mine + pair * e[span(k)].astype(F32) + take * across
        collected(k).start()

    lag = 2

    def tick(lo, hi):
        @pl.when(inner)
        def _():
            loop(lo, hi, combine)
            loop(max(lo - lag, 0), max(hi - lag, 0), pass_on)

    for copy in local:
        copy.wait()

    def project(block):
        r = pl.ds(pl.multiple_of(block * half, half), half)
        tile = min(256, columns)

        def one(k):
            cols = pl.ds(pl.multiple_of(k * tile, tile), tile)
            proj[r, cols] = jnp.dot(a[r, :], w[:, cols], preferred_element_type=F32) * factor
        loop(0, columns // tile, one)

    to_core.wait_recv()
    project(chip)
    tick(0, 1)
    for k in range(parts):
        to_chip(k).wait_recv()
        forward(k).start()
    tick(1, 3)
    for k in range(parts):
        forward(k).wait_recv()
    project(1 - chip)

    group = 128
    groups = tokens // group
    eye = lax.broadcasted_iota(jnp.int32, (group, group), 0) == lax.broadcasted_iota(jnp.int32, (group, group), 1)

    def rows_at(g):
        return pl.ds(pl.multiple_of(g * group, group), group)

    def to_row(column):
        return jnp.sum(jnp.where(eye, column, 0.0), axis=0, keepdims=True)

    def to_column(row):
        return jnp.sum(jnp.where(eye, row, 0.0), axis=1, keepdims=True)

    def exchange(n, k):
        return remote(sent.at[n], sums.at[n, k], ex_s.at[n, k], ex_r.at[n, k], seq=peers[k])

    def post(n):
        for k in range(3):
            exchange(n, k).start()

    def collect(n):
        for k in range(3):
            exchange(n, k).wait_recv()

    def total(n, g):
        one = pl.ds(g, 1)
        return sent[n, one, :] + sums[n, 0, one, :] + sums[n, 1, one, :] + sums[n, 2, one, :]

    def gram_tile(k):
        r = pl.ds(pl.multiple_of(k * 256, 256), 256)
        gram[:, r] = (lax.dot_general(a[...], a[r, :], (((1,), (1,)), ((), ())), preferred_element_type=F32)
                      * (inner_rate / width)).astype(BF16)

    points = ((3, 5), (5, 7), (7, 8), (8, 10), (10, 11), (11, 12))
    for step in range(STEPS):
        first, second = 2 * step, 2 * step + 1

        def squares(g):
            p = proj[rows_at(g), :]
            sent[first, pl.ds(g, 1), :] = to_row(jnp.sum(p * p, axis=1, keepdims=True))
        loop(0, groups, squares)
        post(first)
        if step == 0:
            loop(0, tokens // 256, gram_tile)
        tick(*points[first])
        collect(first)

        def inverse(g):
            return to_column(lax.rsqrt(total(first, g) / width + epsilon))

        def sensitivity(g):
            n = proj[rows_at(g), :] * inverse(g)
            sig = jax.nn.sigmoid(n)
            out = c[rows_at(g), :].astype(F32) * sig * (1.0 + n * (1.0 - sig))
            normed[rows_at(g), :] = n
            sens[rows_at(g), :] = out
            sent[second, pl.ds(g, 1), :] = to_row(jnp.sum(out * n, axis=1, keepdims=True))
        loop(0, groups, sensitivity)
        post(second)
        tick(*points[second])
        collect(second)

        def gradient(g):
            mixed = to_column(total(second, g) / width)
            grads[step, rows_at(g), :] = (
                (sens[rows_at(g), :] - normed[rows_at(g), :] * mixed) * inverse(g)).astype(BF16)
        loop(0, groups, gradient)
        if step < STEPS - 1:
            def descend(k):
                cols = pl.ds(pl.multiple_of(k * 256, 256), 256)
                proj[:, cols] -= jnp.dot(gram[...], grads[step, :, cols], preferred_element_type=F32)
            loop(0, columns // 256, descend)

    def weight_rows(k):
        r = pl.ds(pl.multiple_of(k * 256, 256), 256)
        turned = a[:, r].T
        acc = jnp.dot(turned, grads[0], preferred_element_type=F32)
        for step in range(1, STEPS):
            acc = acc + jnp.dot(turned, grads[step], preferred_element_type=F32)
        cur[r, :] = w[r, :].astype(F32) - acc * (inner_rate * factor)
    loop(0, width // 256, weight_rows)
    trained = pltpu.make_async_copy(cur, cur_hbm, out_s.at[PIECES])
    trained.start()

    @pl.when(inner)
    def _():
        def both(k):
            @pl.when(k < PIECES)
            def _():
                combine(k)
            pass_on(k - lag)
        loop(points[-1][1], PIECES + lag, both)

        def settle(k):
            send_y(k).wait_send()
            send_z(k).wait_send()
        loop(0, PIECES, settle)

    @pl.when(end)
    def _():
        def last(k):
            send_z(k).wait_recv()
            summed[span(k)] = d[span(k)].astype(F32) + e[span(k)].astype(F32)
            collected(k).start()
        loop(0, PIECES, last)
        loop(0, PIECES, lambda k: send_e(k).wait_send())

    tell.wait()
    flag[...] = mark[0] + mark[1]
    to_core.wait_send()
    for k in range(parts):
        to_chip(k).wait_send()
        forward(k).wait_send()
    for n in range(2 * STEPS):
        for k in range(3):
            exchange(n, k).wait_send()

    loop(0, PIECES, lambda k: collected(k).wait())
    trained.wait()


def second_kernel(path, d_hbm, sum_hbm, out_hbm, e, y, add, load, e_s, e_r, y_s, y_r, z_s, z_r, out_s):
    width = y.shape[0]
    rows = width // PIECES
    o = lax.axis_index("outer")
    near = o + 1 - 2 * (o % 2)
    mid = 3 - o
    inner = jnp.logical_or(o == 1, o == 2)
    end = jnp.logical_or(o == 0, o == 3)

    barrier = pltpu.get_barrier_semaphore()
    pl.semaphore_signal(barrier, inc=1, device_id={"outer": near}, device_id_type=MESH)

    @pl.when(inner)
    def _():
        pl.semaphore_signal(barrier, inc=1, device_id={"outer": mid}, device_id_type=MESH)
        pl.semaphore_wait(barrier, 2)

    @pl.when(end)
    def _():
        pl.semaphore_wait(barrier, 1)

    def span(k):
        return pl.ds(pl.multiple_of(k * rows, rows), rows)

    def link(src, dst, send, recv, k, to):
        return pltpu.make_async_remote_copy(
            src_ref=src.at[span(k)], dst_ref=dst.at[span(k)], send_sem=send.at[k], recv_sem=recv.at[k],
            device_id={"outer": to}, device_id_type=MESH)

    def send_e(k):
        return link(d_hbm, e, e_s, e_r, k, near)

    def send_y(k):
        return link(e, y, y_s, y_r, k, mid)

    def send_z(k):
        return link(y, y, z_s, z_r, k, near)

    def loop(lo, hi, body):
        def step(k, carry):
            body(k)
            return carry
        lax.fori_loop(lo, hi, step, 0)

    @pl.when(end)
    def _():
        loop(0, PIECES, lambda k: send_e(k).start())

    fetch = pltpu.make_async_copy(sum_hbm, add, load)
    fetch.start()
    fetch.wait()
    share = second_share(path, o)

    def written(k):
        return pltpu.make_async_copy(add.at[span(k)], out_hbm.at[span(k)], out_s.at[k])

    def take(k):
        add[span(k)] += share * y[span(k)].astype(F32)
        written(k).start()

    @pl.when(inner)
    def _():
        lag = 2

        def relay(k):
            @pl.when(k < PIECES)
            def _():
                send_e(k).wait_recv()
                send_y(k).start()

            @pl.when(k >= lag)
            def _():
                send_y(k - lag).wait_recv()
                send_z(k - lag).start()
                take(k - lag)
        loop(0, PIECES + lag, relay)

        def settle(k):
            send_y(k).wait_send()
            send_z(k).wait_send()
        loop(0, PIECES, settle)

    @pl.when(end)
    def _():
        def last(k):
            send_z(k).wait_recv()
            take(k)
        loop(0, PIECES, last)
        loop(0, PIECES, lambda k: send_e(k).wait_send())

    loop(0, PIECES, lambda k: written(k).wait())


def finish_kernel(path, w, m, cur, summed, new_weights, outer_delta, new_momentum):
    o = lax.axis_index("outer")
    size = same(path, o, 0) + same(path, o, 1) + same(path, o, 2) + same(path, o, 3)
    share = 1.0 / jnp.full((1, w.shape[1]), size, F32)
    outer_grad = summed[...] * share
    moment = beta_outer * m[...].astype(F32) + outer_grad
    direction = outer_grad + beta_outer * moment
    new_momentum[...] = moment.astype(BF16)
    outer_delta[...] = ((w[...].astype(F32) - cur[...]) * (1.0 / (inner_rate * STEPS))).astype(BF16)
    new_weights[...] = (cur[...] - (outer_rate * inner_rate * STEPS) * direction).astype(BF16)


ANY = pl.BlockSpec(memory_space=pl.ANY)
SMEM = pl.BlockSpec(memory_space=pltpu.SMEM)
dma = pltpu.SemaphoreType.DMA


def phase(path, activations, cotangent, weights, earlier_delta):
    width, columns = weights.shape
    tokens = cotangent.shape[0]
    full = pltpu.VMEM((width, columns), BF16)
    wide = pltpu.VMEM((width, columns), F32)
    plane = pltpu.VMEM((tokens, columns), F32)
    line = dma((PIECES,))
    out = jax.ShapeDtypeStruct((width, columns), F32)
    return pl.pallas_call(
        phase_kernel,
        out_shape=(out, out, jax.ShapeDtypeStruct((8, 128), F32)),
        in_specs=[SMEM] + [ANY] * 4,
        out_specs=(ANY, ANY, pl.BlockSpec(memory_space=pltpu.VMEM)),
        scratch_shapes=[
            pltpu.VMEM((tokens, width), BF16), pltpu.VMEM((tokens, columns), BF16),
            full, full, full, full, full, full,
            plane, plane, plane, pltpu.VMEM((tokens, tokens), BF16),
            pltpu.VMEM((STEPS, tokens, columns), BF16), wide, wide,
            pltpu.VMEM((2 * STEPS, 8, 128), F32), pltpu.VMEM((2 * STEPS, 3, 8, 128), F32),
            pltpu.VMEM((2, 8, 128), F32),
            dma((4,)), dma((4,)), dma((4,)), dma, dma, dma((4,)), dma((4,)),
            dma((2 * STEPS, 3)), dma((2 * STEPS, 3)),
            line, line, line, line, line, line, dma((PIECES + 1,)), dma, dma,
        ],
        compiler_params=pltpu.CompilerParams(
            collective_id=1, has_side_effects=True, vmem_limit_bytes=48 * 1024 * 1024),
        cost_estimate=pl.CostEstimate(
            flops=12 * tokens * width * columns, bytes_accessed=14 * width * columns, transcendentals=0),
        name="phase",
    )(path, activations, cotangent, weights, earlier_delta)


def second(path, earlier_delta, summed):
    width, columns = summed.shape
    full = pltpu.VMEM((width, columns), BF16)
    line = dma((PIECES,))
    return pl.pallas_call(
        second_kernel,
        out_shape=jax.ShapeDtypeStruct((width, columns), F32),
        in_specs=[SMEM, ANY, ANY],
        out_specs=ANY,
        scratch_shapes=[full, full, pltpu.VMEM((width, columns), F32), dma] + [line] * 7,
        compiler_params=pltpu.CompilerParams(
            collective_id=2, has_side_effects=True, vmem_limit_bytes=32 * 1024 * 1024),
        name="second",
    )(path, earlier_delta, summed)


def finish(path, weights, momentum, cur, summed):
    width, columns = weights.shape
    rows = 256
    block = pl.BlockSpec((rows, columns), lambda k: (k, 0))
    out = jax.ShapeDtypeStruct((width, columns), BF16)
    return pl.pallas_call(
        finish_kernel,
        grid=(width // rows,),
        out_shape=(out, out, out),
        in_specs=[SMEM, block, block, block, block],
        out_specs=(block, block, block),
        compiler_params=pltpu.CompilerParams(vmem_limit_bytes=24 * 1024 * 1024),
        name="finish",
    )(path, weights, momentum, cur, summed)


def line_body(activations, cotangent, weights, earlier_delta, momentum, module_path):
    delta = earlier_delta[0]
    cur, summed, flag = phase(module_path, activations[0], cotangent[0], weights[0], delta)
    outs = lax.cond(
        flag[0, 0] > 0,
        lambda t: finish(module_path, weights[0], momentum[0], cur, second(module_path, delta, t)),
        lambda t: finish(module_path, weights[0], momentum[0], cur, t),
        summed)
    return tuple(t[None] for t in outs)


def body(activations, cotangent, weights, earlier_delta, momentum, module_path):
    gathered = lax.all_gather(activations[0], "seq", axis=0, tiled=True)
    width = gathered.shape[1]
    factor = 1.0 / jnp.sqrt(jnp.float32(width))
    own_pod = lax.axis_index("outer")
    matches = module_path[:, None] == module_path[None, :]
    shared_bf = jnp.where(matches, 1.0, 0.0).astype(jnp.bfloat16)
    group_size = jnp.sum(jnp.where(matches, 1.0, 0.0).astype(jnp.float32), axis=1)
    own_size = lax.dynamic_index_in_dim(group_size, own_pod, 0, keepdims=False)
    columns = weights.shape[2]
    npods = lax.axis_size("outer")
    blocks = earlier_delta[0].reshape(npods, width // npods, columns)
    sums = jnp.einsum(
        "pq,qrc->prc",
        shared_bf,
        lax.all_to_all(blocks, "outer", split_axis=0, concat_axis=0, tiled=True),
        preferred_element_type=jnp.float32,
    )
    returned = lax.all_to_all(sums, "outer", split_axis=0, concat_axis=0, tiled=True)
    summed = returned.reshape(width, columns)
    outer_grad = summed / own_size
    moment = beta_outer * momentum[0].astype(jnp.float32) + outer_grad
    direction = outer_grad + beta_outer * moment
    sensed = cotangent[0]
    current = weights[0].astype(jnp.float32)
    for inner_step in range(STEPS):
        weight_bf = current.astype(jnp.bfloat16)
        projected = jnp.dot(gathered, weight_bf, preferred_element_type=jnp.float32) * factor
        squares = lax.psum(jnp.sum(projected * projected, axis=1), "seq")
        row_rms = jnp.sqrt(squares / width + epsilon)[:, None]
        normed = projected / row_rms
        sigmoid_y = jax.nn.sigmoid(normed)
        grad_out = sensed.astype(jnp.float32) * sigmoid_y * (1.0 + normed * (1.0 - sigmoid_y))
        products = lax.psum(jnp.sum(grad_out * normed, axis=1), "seq")
        grad_in = ((grad_out - normed * (products / width)[:, None]) / row_rms).astype(jnp.bfloat16)
        gradient = (
            lax.dot_general(
                gathered, grad_in, (((0,), (0,)), ((), ())), preferred_element_type=jnp.float32
            )
            * factor
        )
        current = current - inner_rate * gradient
    outer_delta = ((weights[0].astype(jnp.float32) - current) / (inner_rate * STEPS)).astype(
        jnp.bfloat16
    )
    new_weights = (current - outer_rate * inner_rate * STEPS * direction).astype(jnp.bfloat16)
    new_momentum = moment.astype(jnp.bfloat16)
    return (new_weights[None], outer_delta[None], new_momentum[None])


def solution(mesh):
    in_specs = (
        P(("group", "outer"), "seq", None),
        P(("group", "outer"), None, "seq"),
        P(("group", "outer"), None, "seq"),
        P(("group", "outer"), None, "seq"),
        P(("group", "outer"), None, "seq"),
        P("group"),
    )
    out_specs = (
        P(("group", "outer"), None, "seq"),
        P(("group", "outer"), None, "seq"),
        P(("group", "outer"), None, "seq"),
    )
    def run(*args):
        sizes = (mesh.shape["outer"], mesh.shape["seq"], args[0].shape[1], args[2].shape[1])
        fits = mesh.shape["group"] == 2 and sizes[:2] == (4, 4) and sizes[2] == 512 and sizes[3] % 512 == 0 and sizes[3] <= 2048
        chosen = line_body if fits else body
        return jax.shard_map(
            chosen, mesh=mesh, in_specs=in_specs, out_specs=out_specs, check_vma=False)(*args)

    return run
```

```python
import functools

import jax
import jax.numpy as jnp
from jax import lax
from jax.experimental import pallas as pl
from jax.experimental.pallas import tpu as pltpu
from jax.sharding import PartitionSpec as P

STEPS = 3


epsilon = 1e-06
inner_rate = 0.05
outer_rate = 0.7
beta_outer = 0.9

MESH = pl.DeviceIdType.MESH
PIECES = 32
F32 = jnp.float32
BF16 = jnp.bfloat16


def same(path, i, j):
    return jnp.where(path[i] == path[j], 1.0, 0.0)


def crossing(path, i):
    other = 2 - 2 * (i // 2)
    return jnp.maximum(same(path, i, other), same(path, i, other + 1))


def others(i):
    low = i // 2
    return 2 - low, 3 - 3 * low


def first_share(path, i):
    near, far = others(i)
    inner = crossing(path, near)
    return inner * same(path, i, near) + (1.0 - inner) * same(path, i, far)


def second_share(path, i):
    near, far = others(i)
    return crossing(path, near) * (1.0 - same(path, near, far)) * same(path, i, far)


def phase_kernel(path, a_hbm, c_hbm, w_hbm, d_hbm, cur_hbm, sum_hbm, flag,
                 a, c, w, d, e, x, y, z, proj, normed, sens, gram, grads, cur, summed,
                 sent, sums, mark, load, agx_s, agx_r, agc_s, agc_r, agf_s, agf_r, ex_s, ex_r,
                 e_s, e_r, y_s, y_r, z_s, z_r, out_s, mark_s, mark_r):
    tokens, width = a.shape
    columns = w.shape[1]
    shard = tokens // 4
    half = tokens // 2
    rows = width // PIECES
    factor = 1.0 / width ** 0.5

    o = lax.axis_index("outer")
    s = lax.axis_index("seq")
    part = lax.axis_index("group")
    core = s % 2
    chip = s // 2
    peers = (chip * 2 + 1 - core, (1 - chip) * 2 + core, (1 - chip) * 2 + 1 - core)
    near = o + 1 - 2 * (o % 2)
    mid = 3 - o
    inner = jnp.logical_or(o == 1, o == 2)
    end = jnp.logical_or(o == 0, o == 3)

    def remote(src, dst, send, recv, **where):
        return pltpu.make_async_remote_copy(
            src_ref=src, dst_ref=dst, send_sem=send, recv_sem=recv, device_id=where, device_id_type=MESH)

    barrier = pltpu.get_barrier_semaphore()
    for peer in peers:
        pl.semaphore_signal(barrier, inc=1, device_id={"seq": peer}, device_id_type=MESH)
    pl.semaphore_signal(barrier, inc=1, device_id={"outer": near}, device_id_type=MESH)
    pl.semaphore_signal(barrier, inc=1, device_id={"group": 1 - part}, device_id_type=MESH)

    @pl.when(inner)
    def _():
        pl.semaphore_signal(barrier, inc=1, device_id={"outer": mid}, device_id_type=MESH)

    local = [pltpu.make_async_copy(x, y, load.at[k]) for k, (x, y) in enumerate(
        ((a_hbm, a.at[pl.ds(pl.multiple_of(s * shard, shard), shard)]), (w_hbm, w), (c_hbm, c), (d_hbm, d)))]
    for copy in local:
        copy.start()

    @pl.when(inner)
    def _():
        pl.semaphore_wait(barrier, 6)

    @pl.when(end)
    def _():
        pl.semaphore_wait(barrier, 5)

    parts = 4
    piece = shard // parts

    def rows_of(owner, k):
        return pl.ds(pl.multiple_of(owner * shard + k * piece, piece), piece)

    def to_chip(k):
        return remote(a_hbm.at[pl.ds(k * piece, piece)], a.at[rows_of(s, k)], agx_s.at[k], agx_r.at[k], seq=peers[1])

    def forward(k):
        return remote(a.at[rows_of(peers[1], k)], a.at[rows_of(peers[1], k)], agf_s.at[k], agf_r.at[k], seq=peers[0])

    own_rows = pl.ds(pl.multiple_of(s * shard, shard), shard)
    to_core = remote(a_hbm, a.at[own_rows], agc_s, agc_r, seq=peers[0])
    for k in range(parts):
        to_chip(k).start()
    to_core.start()

    def span(k):
        return pl.ds(pl.multiple_of(k * rows, rows), rows)

    def send_e(k):
        return remote(d_hbm.at[span(k)], e.at[span(k)], e_s.at[k], e_r.at[k], outer=near)

    def send_y(k):
        return remote(x.at[span(k)], y.at[span(k)], y_s.at[k], y_r.at[k], outer=mid)

    def send_z(k):
        return remote(z.at[span(k)], e.at[span(k)], z_s.at[k], z_r.at[k], outer=near)

    def loop(lo, hi, body):
        def step(k, carry):
            body(k)
            return carry
        lax.fori_loop(lo, hi, step, 0)

    @pl.when(end)
    def _():
        loop(0, PIECES, lambda k: send_e(k).start())

    need = crossing(path, 0) * crossing(path, 1) * (1.0 - same(path, 0, 1))
    mark[0] = jnp.full((8, 128), need, F32)
    tell = remote(mark.at[0], mark.at[1], mark_s, mark_r, group=1 - part)
    tell.start()

    own_cross = crossing(path, o)
    x_own = own_cross
    x_end = own_cross * same(path, o, near) + (1.0 - own_cross) * crossing(path, near)
    pair = same(path, o, near)
    take = first_share(path, o)
    near_take = first_share(path, near)

    def collected(k):
        return pltpu.make_async_copy(summed.at[span(k)], sum_hbm.at[span(k)], out_s.at[k])

    def combine(k):
        send_e(k).wait_recv()
        x[span(k)] = (x_end * e[span(k)].astype(F32) + x_own * d[span(k)].astype(F32)).astype(BF16)
        send_y(k).start()

    def pass_on(k):
        send_y(k).wait_recv()
        mine = d[span(k)].astype(F32)
        across = y[span(k)].astype(F32)
        z[span(k)] = (pair * mine + near_take * across).astype(BF16)
        send_z(k).start()
        summed[span(k)] = mine + pair * e[span(k)].astype(F32) + take * across
        collected(k).start()

    lag = 4

    def tick(lo, hi):
        @pl.when(inner)
        def _():
            loop(lo, hi, combine)
            loop(max(lo - lag, 0), max(hi - lag, 0), pass_on)

    for copy in local:
        copy.wait()

    def project(block):
        r = pl.ds(pl.multiple_of(block * half, half), half)
        tile = min(256, columns)

        def one(k):
            cols = pl.ds(pl.multiple_of(k * tile, tile), tile)
            proj[r, cols] = jnp.dot(a[r, :], w[:, cols], preferred_element_type=F32) * factor
        loop(0, columns // tile, one)

    to_core.wait_recv()
    project(chip)
    tick(0, 2)
    for k in range(parts):
        to_chip(k).wait_recv()
        forward(k).start()
    tick(2, 6)
    for k in range(parts):
        forward(k).wait_recv()
    project(1 - chip)

    group = 128
    groups = tokens // group
    eye = lax.broadcasted_iota(jnp.int32, (group, group), 0) == lax.broadcasted_iota(jnp.int32, (group, group), 1)

    def rows_at(g):
        return pl.ds(pl.multiple_of(g * group, group), group)

    def to_row(column):
        return jnp.sum(jnp.where(eye, column, 0.0), axis=0, keepdims=True)

    def to_column(row):
        return jnp.sum(jnp.where(eye, row, 0.0), axis=1, keepdims=True)

    def exchange(n, k):
        return remote(sent.at[n], sums.at[n, k], ex_s.at[n, k], ex_r.at[n, k], seq=peers[k])

    def post(n):
        for k in range(3):
            exchange(n, k).start()

    def collect(n):
        for k in range(3):
            exchange(n, k).wait_recv()

    def total(n, g):
        one = pl.ds(g, 1)
        return sent[n, one, :] + sums[n, 0, one, :] + sums[n, 1, one, :] + sums[n, 2, one, :]

    def gram_tile(k):
        r = pl.ds(pl.multiple_of(k * 256, 256), 256)
        gram[:, r] = (lax.dot_general(a[...], a[r, :], (((1,), (1,)), ((), ())), preferred_element_type=F32)
                      * (inner_rate / width)).astype(BF16)

    points = ((6, 10), (10, 14), (14, 18), (18, 21), (21, 25), (25, 28))
    for step in range(STEPS):
        first, second = 2 * step, 2 * step + 1

        def squares(g):
            p = proj[rows_at(g), :]
            sent[first, pl.ds(g, 1), :] = to_row(jnp.sum(p * p, axis=1, keepdims=True))
        loop(0, groups, squares)
        post(first)
        if step == 0:
            loop(0, tokens // 256, gram_tile)
        tick(*points[first])
        collect(first)

        def inverse(g):
            return to_column(lax.rsqrt(total(first, g) / width + epsilon))

        def sensitivity(g):
            n = proj[rows_at(g), :] * inverse(g)
            sig = jax.nn.sigmoid(n)
            out = c[rows_at(g), :].astype(F32) * sig * (1.0 + n * (1.0 - sig))
            normed[rows_at(g), :] = n
            sens[rows_at(g), :] = out
            sent[second, pl.ds(g, 1), :] = to_row(jnp.sum(out * n, axis=1, keepdims=True))
        loop(0, groups, sensitivity)
        post(second)
        tick(*points[second])
        collect(second)

        def gradient(g):
            mixed = to_column(total(second, g) / width)
            grads[step, rows_at(g), :] = (
                (sens[rows_at(g), :] - normed[rows_at(g), :] * mixed) * inverse(g)).astype(BF16)
        loop(0, groups, gradient)
        if step < STEPS - 1:
            def descend(k):
                cols = pl.ds(pl.multiple_of(k * 256, 256), 256)
                proj[:, cols] -= jnp.dot(gram[...], grads[step, :, cols], preferred_element_type=F32)
            loop(0, columns // 256, descend)

    def weight_rows(k):
        r = pl.ds(pl.multiple_of(k * 256, 256), 256)
        turned = a[:, r].T
        acc = jnp.dot(turned, grads[0], preferred_element_type=F32)
        for step in range(1, STEPS):
            acc = acc + jnp.dot(turned, grads[step], preferred_element_type=F32)
        cur[r, :] = w[r, :].astype(F32) - acc * (inner_rate * factor)

        @pl.when(jnp.logical_and(inner, k % 2 == 1))
        def _():
            combine(points[-1][1] + k // 2)
            pass_on(points[-1][1] + k // 2 - lag)
    loop(0, width // 256, weight_rows)
    trained = pltpu.make_async_copy(cur, cur_hbm, out_s.at[PIECES])
    trained.start()

    @pl.when(inner)
    def _():
        def both(k):
            @pl.when(k < PIECES)
            def _():
                combine(k)
            pass_on(k - lag)
        loop(points[-1][1] + width // 512, PIECES + lag, both)

        def settle(k):
            send_y(k).wait_send()
            send_z(k).wait_send()
        loop(0, PIECES, settle)

    @pl.when(end)
    def _():
        def last(k):
            send_z(k).wait_recv()
            summed[span(k)] = d[span(k)].astype(F32) + e[span(k)].astype(F32)
            collected(k).start()
        loop(0, PIECES, last)
        loop(0, PIECES, lambda k: send_e(k).wait_send())

    tell.wait()
    flag[...] = mark[0] + mark[1]
    to_core.wait_send()
    for k in range(parts):
        to_chip(k).wait_send()
        forward(k).wait_send()
    for n in range(2 * STEPS):
        for k in range(3):
            exchange(n, k).wait_send()

    loop(0, PIECES, lambda k: collected(k).wait())
    trained.wait()


def second_kernel(path, d_hbm, sum_hbm, out_hbm, e, y, add, load, e_s, e_r, y_s, y_r, z_s, z_r, out_s):
    width = y.shape[0]
    rows = width // PIECES
    o = lax.axis_index("outer")
    near = o + 1 - 2 * (o % 2)
    mid = 3 - o
    inner = jnp.logical_or(o == 1, o == 2)
    end = jnp.logical_or(o == 0, o == 3)

    barrier = pltpu.get_barrier_semaphore()
    pl.semaphore_signal(barrier, inc=1, device_id={"outer": near}, device_id_type=MESH)

    @pl.when(inner)
    def _():
        pl.semaphore_signal(barrier, inc=1, device_id={"outer": mid}, device_id_type=MESH)
        pl.semaphore_wait(barrier, 2)

    @pl.when(end)
    def _():
        pl.semaphore_wait(barrier, 1)

    def span(k):
        return pl.ds(pl.multiple_of(k * rows, rows), rows)

    def link(src, dst, send, recv, k, to):
        return pltpu.make_async_remote_copy(
            src_ref=src.at[span(k)], dst_ref=dst.at[span(k)], send_sem=send.at[k], recv_sem=recv.at[k],
            device_id={"outer": to}, device_id_type=MESH)

    def send_e(k):
        return link(d_hbm, e, e_s, e_r, k, near)

    def send_y(k):
        return link(e, y, y_s, y_r, k, mid)

    def send_z(k):
        return link(y, y, z_s, z_r, k, near)

    def loop(lo, hi, body):
        def step(k, carry):
            body(k)
            return carry
        lax.fori_loop(lo, hi, step, 0)

    @pl.when(end)
    def _():
        loop(0, PIECES, lambda k: send_e(k).start())

    fetch = pltpu.make_async_copy(sum_hbm, add, load)
    fetch.start()
    fetch.wait()
    share = second_share(path, o)

    def written(k):
        return pltpu.make_async_copy(add.at[span(k)], out_hbm.at[span(k)], out_s.at[k])

    def take(k):
        add[span(k)] += share * y[span(k)].astype(F32)
        written(k).start()

    @pl.when(inner)
    def _():
        lag = 2

        def relay(k):
            @pl.when(k < PIECES)
            def _():
                send_e(k).wait_recv()
                send_y(k).start()

            @pl.when(k >= lag)
            def _():
                send_y(k - lag).wait_recv()
                send_z(k - lag).start()
                take(k - lag)
        loop(0, PIECES + lag, relay)

        def settle(k):
            send_y(k).wait_send()
            send_z(k).wait_send()
        loop(0, PIECES, settle)

    @pl.when(end)
    def _():
        def last(k):
            send_z(k).wait_recv()
            take(k)
        loop(0, PIECES, last)
        loop(0, PIECES, lambda k: send_e(k).wait_send())

    loop(0, PIECES, lambda k: written(k).wait())


def finish_kernel(path, w, m, cur, summed, nw_hbm, od_hbm, nm_hbm, nw, od, nm, sems):
    o = lax.axis_index("outer")
    size = same(path, o, 0) + same(path, o, 1) + same(path, o, 2) + same(path, o, 3)
    share = 1.0 / jnp.full((1, w.shape[1]), size, F32)
    rows = w.shape[0] // 16

    def outs(k):
        r = pl.ds(pl.multiple_of(k * rows, rows), rows)
        return [pltpu.make_async_copy(x.at[r], y.at[r], sems.at[n, k])
                for n, (x, y) in enumerate(((nw, nw_hbm), (od, od_hbm), (nm, nm_hbm)))]

    def step(k, carry):
        r = pl.ds(pl.multiple_of(k * rows, rows), rows)
        outer_grad = summed[r] * share
        moment = beta_outer * m[r].astype(F32) + outer_grad
        direction = outer_grad + beta_outer * moment
        nm[r] = moment.astype(BF16)
        od[r] = ((w[r].astype(F32) - cur[r]) * (1.0 / (inner_rate * STEPS))).astype(BF16)
        nw[r] = (cur[r] - (outer_rate * inner_rate * STEPS) * direction).astype(BF16)
        for copy in outs(k):
            copy.start()
        return carry
    lax.fori_loop(0, 16, step, 0)

    def settle(k, carry):
        for copy in outs(k):
            copy.wait()
        return carry
    lax.fori_loop(0, 16, settle, 0)


ANY = pl.BlockSpec(memory_space=pl.ANY)
HBM = pl.BlockSpec(memory_space=pltpu.HBM)
SMEM = pl.BlockSpec(memory_space=pltpu.SMEM)
dma = pltpu.SemaphoreType.DMA


def phase(path, activations, cotangent, weights, earlier_delta):
    width, columns = weights.shape
    tokens = cotangent.shape[0]
    full = pltpu.VMEM((width, columns), BF16)
    wide = pltpu.VMEM((width, columns), F32)
    plane = pltpu.VMEM((tokens, columns), F32)
    line = dma((PIECES,))
    out = jax.ShapeDtypeStruct((width, columns), F32)
    return pl.pallas_call(
        phase_kernel,
        out_shape=(out, out, jax.ShapeDtypeStruct((8, 128), F32)),
        in_specs=[SMEM] + [HBM] * 4,
        out_specs=(ANY, ANY, pl.BlockSpec(memory_space=pltpu.VMEM)),
        scratch_shapes=[
            pltpu.VMEM((tokens, width), BF16), pltpu.VMEM((tokens, columns), BF16),
            full, full, full, full, full, full,
            plane, plane, plane, pltpu.VMEM((tokens, tokens), BF16),
            pltpu.VMEM((STEPS, tokens, columns), BF16), wide, wide,
            pltpu.VMEM((2 * STEPS, 8, 128), F32), pltpu.VMEM((2 * STEPS, 3, 8, 128), F32),
            pltpu.VMEM((2, 8, 128), F32),
            dma((4,)), dma((4,)), dma((4,)), dma, dma, dma((4,)), dma((4,)),
            dma((2 * STEPS, 3)), dma((2 * STEPS, 3)),
            line, line, line, line, line, line, dma((PIECES + 1,)), dma, dma,
        ],
        compiler_params=pltpu.CompilerParams(
            collective_id=1, has_side_effects=True, vmem_limit_bytes=48 * 1024 * 1024),
        cost_estimate=pl.CostEstimate(
            flops=12 * tokens * width * columns, bytes_accessed=14 * width * columns, transcendentals=0),
        name="phase",
    )(path, activations, cotangent, weights, earlier_delta)


def second(path, earlier_delta, summed):
    width, columns = summed.shape
    full = pltpu.VMEM((width, columns), BF16)
    line = dma((PIECES,))
    return pl.pallas_call(
        second_kernel,
        out_shape=jax.ShapeDtypeStruct((width, columns), F32),
        in_specs=[SMEM, ANY, ANY],
        out_specs=ANY,
        scratch_shapes=[full, full, pltpu.VMEM((width, columns), F32), dma] + [line] * 7,
        compiler_params=pltpu.CompilerParams(
            collective_id=2, has_side_effects=True, vmem_limit_bytes=32 * 1024 * 1024),
        name="second",
    )(path, earlier_delta, summed)


def finish(path, weights, momentum, cur, summed):
    width, columns = weights.shape
    out = jax.ShapeDtypeStruct((width, columns), BF16)
    return pl.pallas_call(
        finish_kernel,
        out_shape=(out, out, out),
        in_specs=[SMEM] + [pl.BlockSpec(memory_space=pltpu.VMEM)] * 4,
        out_specs=(HBM,) * 3,
        scratch_shapes=[pltpu.VMEM((width, columns), BF16)] * 3 + [dma((3, 16))],
        compiler_params=pltpu.CompilerParams(vmem_limit_bytes=32 * 1024 * 1024),
        name="finish",
    )(path, weights, momentum, cur, summed)


def line_body(activations, cotangent, weights, earlier_delta, momentum, module_path):
    delta = earlier_delta[0]
    cur, summed, flag = phase(module_path, activations[0], cotangent[0], weights[0], delta)
    outs = lax.cond(
        flag[0, 0] > 0,
        lambda t: finish(module_path, weights[0], momentum[0], cur, second(module_path, delta, t)),
        lambda t: finish(module_path, weights[0], momentum[0], cur, t),
        summed)
    return tuple(t[None] for t in outs)


def body(activations, cotangent, weights, earlier_delta, momentum, module_path):
    gathered = lax.all_gather(activations[0], "seq", axis=0, tiled=True)
    width = gathered.shape[1]
    factor = 1.0 / jnp.sqrt(jnp.float32(width))
    own_pod = lax.axis_index("outer")
    matches = module_path[:, None] == module_path[None, :]
    shared_bf = jnp.where(matches, 1.0, 0.0).astype(jnp.bfloat16)
    group_size = jnp.sum(jnp.where(matches, 1.0, 0.0).astype(jnp.float32), axis=1)
    own_size = lax.dynamic_index_in_dim(group_size, own_pod, 0, keepdims=False)
    columns = weights.shape[2]
    npods = lax.axis_size("outer")
    blocks = earlier_delta[0].reshape(npods, width // npods, columns)
    sums = jnp.einsum(
        "pq,qrc->prc",
        shared_bf,
        lax.all_to_all(blocks, "outer", split_axis=0, concat_axis=0, tiled=True),
        preferred_element_type=jnp.float32,
    )
    returned = lax.all_to_all(sums, "outer", split_axis=0, concat_axis=0, tiled=True)
    summed = returned.reshape(width, columns)
    outer_grad = summed / own_size
    moment = beta_outer * momentum[0].astype(jnp.float32) + outer_grad
    direction = outer_grad + beta_outer * moment
    sensed = cotangent[0]
    current = weights[0].astype(jnp.float32)
    for inner_step in range(STEPS):
        weight_bf = current.astype(jnp.bfloat16)
        projected = jnp.dot(gathered, weight_bf, preferred_element_type=jnp.float32) * factor
        squares = lax.psum(jnp.sum(projected * projected, axis=1), "seq")
        row_rms = jnp.sqrt(squares / width + epsilon)[:, None]
        normed = projected / row_rms
        sigmoid_y = jax.nn.sigmoid(normed)
        grad_out = sensed.astype(jnp.float32) * sigmoid_y * (1.0 + normed * (1.0 - sigmoid_y))
        products = lax.psum(jnp.sum(grad_out * normed, axis=1), "seq")
        grad_in = ((grad_out - normed * (products / width)[:, None]) / row_rms).astype(jnp.bfloat16)
        gradient = (
            lax.dot_general(
                gathered, grad_in, (((0,), (0,)), ((), ())), preferred_element_type=jnp.float32
            )
            * factor
        )
        current = current - inner_rate * gradient
    outer_delta = ((weights[0].astype(jnp.float32) - current) / (inner_rate * STEPS)).astype(
        jnp.bfloat16
    )
    new_weights = (current - outer_rate * inner_rate * STEPS * direction).astype(jnp.bfloat16)
    new_momentum = moment.astype(jnp.bfloat16)
    return (new_weights[None], outer_delta[None], new_momentum[None])


def solution(mesh):
    in_specs = (
        P(("group", "outer"), "seq", None),
        P(("group", "outer"), None, "seq"),
        P(("group", "outer"), None, "seq"),
        P(("group", "outer"), None, "seq"),
        P(("group", "outer"), None, "seq"),
        P("group"),
    )
    out_specs = (
        P(("group", "outer"), None, "seq"),
        P(("group", "outer"), None, "seq"),
        P(("group", "outer"), None, "seq"),
    )
    def run(*args):
        sizes = (mesh.shape["outer"], mesh.shape["seq"], args[0].shape[1], args[2].shape[1])
        fits = mesh.shape["group"] == 2 and sizes[:2] == (4, 4) and sizes[2] == 512 and sizes[3] % 512 == 0 and sizes[3] <= 2048
        chosen = line_body if fits else body
        return jax.shard_map(
            chosen, mesh=mesh, in_specs=in_specs, out_specs=out_specs, check_vma=False)(*args)

    return run
```

```python
import functools

import jax
import jax.numpy as jnp
from jax import lax
from jax.experimental import pallas as pl
from jax.experimental.pallas import tpu as pltpu
from jax.sharding import PartitionSpec as P

STEPS = 3


epsilon = 1e-06
inner_rate = 0.05
outer_rate = 0.7
beta_outer = 0.9

MESH = pl.DeviceIdType.MESH
FIRST = (2, 2, 4)
EVEN = 13
LAST = (4, 4, 2, 2, 2, 2)
HEAD = len(FIRST)
TAIL = HEAD + EVEN
PIECES = TAIL + len(LAST)
F32 = jnp.float32
BF16 = jnp.bfloat16


def loop(lo, hi, body):
    def step(k, carry):
        body(k)
        return carry
    for k in range(lo, min(hi, HEAD)):
        body(k)
    if max(lo, HEAD) < min(hi, TAIL):
        lax.fori_loop(max(lo, HEAD), min(hi, TAIL), step, 0)
    for k in range(max(lo, TAIL), hi):
        body(k)


def repeat(count, body):
    def step(k, carry):
        body(k)
        return carry
    lax.fori_loop(0, count, step, 0)


def span_of(width, k):
    rows = width // (EVEN + (sum(FIRST) + sum(LAST)) // 8)
    sizes = FIRST + (8,) * EVEN + LAST
    if isinstance(k, int):
        return pl.ds(sum(sizes[:k]) * rows // 8, sizes[k] * rows // 8)
    return pl.ds(pl.multiple_of((k - HEAD) * rows + sum(FIRST) * rows // 8, rows), rows)


def same(path, i, j):
    return jnp.where(path[i] == path[j], 1.0, 0.0)


def crossing(path, i):
    other = 2 - 2 * (i // 2)
    return jnp.maximum(same(path, i, other), same(path, i, other + 1))


def others(i):
    low = i // 2
    return 2 - low, 3 - 3 * low


def first_share(path, i):
    near, far = others(i)
    inner = crossing(path, near)
    return inner * same(path, i, near) + (1.0 - inner) * same(path, i, far)


def second_share(path, i):
    near, far = others(i)
    return crossing(path, near) * (1.0 - same(path, near, far)) * same(path, i, far)


def phase_kernel(path, a_hbm, c_hbm, w_hbm, d_hbm, cur_hbm, sum_hbm, flag,
                 a, c, w, d, e, x, y, z, proj, normed, sens, gram, grads, cur, summed,
                 sent, sums, mark, load, agx_s, agx_r, agc_s, agc_r, agf_s, agf_r, ex_s, ex_r,
                 e_s, e_r, y_s, y_r, z_s, z_r, out_s, mark_s, mark_r):
    tokens, width = a.shape
    columns = w.shape[1]
    shard = tokens // 4
    half = tokens // 2
    factor = 1.0 / width ** 0.5

    o = lax.axis_index("outer")
    s = lax.axis_index("seq")
    part = lax.axis_index("group")
    core = s % 2
    chip = s // 2
    peers = (chip * 2 + 1 - core, (1 - chip) * 2 + core, (1 - chip) * 2 + 1 - core)
    near = o + 1 - 2 * (o % 2)
    mid = 3 - o
    inner = jnp.logical_or(o == 1, o == 2)
    end = jnp.logical_or(o == 0, o == 3)

    def remote(src, dst, send, recv, **where):
        return pltpu.make_async_remote_copy(
            src_ref=src, dst_ref=dst, send_sem=send, recv_sem=recv, device_id=where, device_id_type=MESH)

    barrier = pltpu.get_barrier_semaphore()
    for peer in peers:
        pl.semaphore_signal(barrier, inc=1, device_id={"seq": peer}, device_id_type=MESH)
    pl.semaphore_signal(barrier, inc=1, device_id={"outer": near}, device_id_type=MESH)
    pl.semaphore_signal(barrier, inc=1, device_id={"group": 1 - part}, device_id_type=MESH)

    @pl.when(inner)
    def _():
        pl.semaphore_signal(barrier, inc=1, device_id={"outer": mid}, device_id_type=MESH)

    local = [pltpu.make_async_copy(x, y, load.at[k]) for k, (x, y) in enumerate(
        ((a_hbm, a.at[pl.ds(pl.multiple_of(s * shard, shard), shard)]), (w_hbm, w), (c_hbm, c), (d_hbm, d)))]
    for copy in local:
        copy.start()

    @pl.when(inner)
    def _():
        pl.semaphore_wait(barrier, 6)

    @pl.when(end)
    def _():
        pl.semaphore_wait(barrier, 5)

    parts = 4
    piece = shard // parts

    def rows_of(owner, k):
        return pl.ds(pl.multiple_of(owner * shard + k * piece, piece), piece)

    def to_chip(k):
        return remote(a_hbm.at[pl.ds(k * piece, piece)], a.at[rows_of(s, k)], agx_s.at[k], agx_r.at[k], seq=peers[1])

    def forward(k):
        return remote(a.at[rows_of(peers[1], k)], a.at[rows_of(peers[1], k)], agf_s.at[k], agf_r.at[k], seq=peers[0])

    own_rows = pl.ds(pl.multiple_of(s * shard, shard), shard)
    to_core = remote(a_hbm, a.at[own_rows], agc_s, agc_r, seq=peers[0])
    for k in range(parts):
        to_chip(k).start()
    to_core.start()

    def span(k):
        return span_of(width, k)

    def send_e(k):
        return remote(d_hbm.at[span(k)], e.at[span(k)], e_s.at[k], e_r.at[k], outer=near)

    def send_y(k):
        return remote(x.at[span(k)], y.at[span(k)], y_s.at[k], y_r.at[k], outer=mid)

    def send_z(k):
        return remote(z.at[span(k)], e.at[span(k)], z_s.at[k], z_r.at[k], outer=near)

    @pl.when(end)
    def _():
        loop(0, PIECES, lambda k: send_e(k).start())

    need = crossing(path, 0) * crossing(path, 1) * (1.0 - same(path, 0, 1))
    mark[0] = jnp.full((8, 128), need, F32)
    tell = remote(mark.at[0], mark.at[1], mark_s, mark_r, group=1 - part)
    tell.start()

    own_cross = crossing(path, o)
    x_own = own_cross
    x_end = own_cross * same(path, o, near) + (1.0 - own_cross) * crossing(path, near)
    pair = same(path, o, near)
    take = first_share(path, o)
    near_take = first_share(path, near)

    def collected(k):
        return pltpu.make_async_copy(summed.at[span(k)], sum_hbm.at[span(k)], out_s.at[k])

    def combine(k):
        send_e(k).wait_recv()
        x[span(k)] = (x_end * e[span(k)].astype(F32) + x_own * d[span(k)].astype(F32)).astype(BF16)
        send_y(k).start()

    def pass_on(k):
        send_y(k).wait_recv()
        mine = d[span(k)].astype(F32)
        across = y[span(k)].astype(F32)
        z[span(k)] = (pair * mine + near_take * across).astype(BF16)
        send_z(k).start()
        summed[span(k)] = mine + pair * e[span(k)].astype(F32) + take * across
        collected(k).start()

    lag = 2

    place = [0]

    def tick(count):
        lo, hi = place[0], place[0] + count
        place[0] = hi

        @pl.when(inner)
        def _():
            loop(lo, min(hi, PIECES), combine)
            loop(max(lo - lag, 0), max(hi - lag, 0), pass_on)

    for copy in local:
        copy.wait()

    def project(block):
        r = pl.ds(pl.multiple_of(block * half, half), half)
        tile = min(256, columns)

        def one(k):
            cols = pl.ds(pl.multiple_of(k * tile, tile), tile)
            proj[r, cols] = jnp.dot(a[r, :], w[:, cols], preferred_element_type=F32) * factor
        repeat(columns // tile, one)

    to_core.wait_recv()
    tick(2)
    project(chip)
    tick(2)
    for k in range(parts):
        to_chip(k).wait_recv()
        forward(k).start()
        if k % 2 == 0:
            tick(1)
    tick(1)
    for k in range(parts):
        forward(k).wait_recv()
    project(1 - chip)
    tick(1)

    group = 128
    groups = tokens // group
    eye = lax.broadcasted_iota(jnp.int32, (group, group), 0) == lax.broadcasted_iota(jnp.int32, (group, group), 1)

    def rows_at(g):
        return pl.ds(pl.multiple_of(g * group, group), group)

    def to_row(column):
        return jnp.sum(jnp.where(eye, column, 0.0), axis=0, keepdims=True)

    def to_column(row):
        return jnp.sum(jnp.where(eye, row, 0.0), axis=1, keepdims=True)

    def exchange(n, k):
        return remote(sent.at[n], sums.at[n, k], ex_s.at[n, k], ex_r.at[n, k], seq=peers[k])

    def post(n):
        for k in range(3):
            exchange(n, k).start()

    def collect(n):
        for k in range(3):
            exchange(n, k).wait_recv()

    def total(n, g):
        one = pl.ds(g, 1)
        return sent[n, one, :] + sums[n, 0, one, :] + sums[n, 1, one, :] + sums[n, 2, one, :]

    def gram_tile(k):
        r = pl.ds(pl.multiple_of(k * 256, 256), 256)
        gram[:, r] = (lax.dot_general(a[...], a[r, :], (((1,), (1,)), ((), ())), preferred_element_type=F32)
                      * (inner_rate / width)).astype(BF16)

    for step in range(STEPS):
        first, second = 2 * step, 2 * step + 1

        def squares(g):
            p = proj[rows_at(g), :]
            sent[first, pl.ds(g, 1), :] = to_row(jnp.sum(p * p, axis=1, keepdims=True))
        repeat(groups, squares)
        post(first)
        if step == 0:
            repeat(tokens // 256, gram_tile)
        tick(1)
        collect(first)

        def inverse(g):
            return to_column(lax.rsqrt(total(first, g) / width + epsilon))

        def sensitivity(g):
            n = proj[rows_at(g), :] * inverse(g)
            sig = jax.nn.sigmoid(n)
            out = c[rows_at(g), :].astype(F32) * sig * (1.0 + n * (1.0 - sig))
            normed[rows_at(g), :] = n
            sens[rows_at(g), :] = out
            sent[second, pl.ds(g, 1), :] = to_row(jnp.sum(out * n, axis=1, keepdims=True))
        repeat(groups, sensitivity)
        post(second)
        tick(1)
        collect(second)

        def gradient(g):
            mixed = to_column(total(second, g) / width)
            grads[step, rows_at(g), :] = (
                (sens[rows_at(g), :] - normed[rows_at(g), :] * mixed) * inverse(g)).astype(BF16)
        repeat(groups, gradient)
        if step < STEPS - 1:
            def descend(k):
                cols = pl.ds(pl.multiple_of(k * 256, 256), 256)
                proj[:, cols] -= jnp.dot(gram[...], grads[step, :, cols], preferred_element_type=F32)
            repeat(columns // 256, descend)
        tick(1)

    def weight_rows(k):
        r = pl.ds(pl.multiple_of(k * 256, 256), 256)
        turned = a[:, r].T
        acc = jnp.dot(turned, grads[0], preferred_element_type=F32)
        for step in range(1, STEPS):
            acc = acc + jnp.dot(turned, grads[step], preferred_element_type=F32)
        cur[r, :] = w[r, :].astype(F32) - acc * (inner_rate * factor)

    for quarter in range(4):
        repeat(width // 1024, lambda k: weight_rows(quarter * (width // 1024) + k))
        tick(1)
    trained = pltpu.make_async_copy(cur, cur_hbm, out_s.at[PIECES])
    trained.start()

    @pl.when(inner)
    def _():
        for k in range(place[0], PIECES + lag):
            if k < PIECES:
                combine(k)
            pass_on(k - lag)

        def settle(k):
            send_y(k).wait_send()
            send_z(k).wait_send()
        loop(0, PIECES, settle)

    @pl.when(end)
    def _():
        def last(k):
            send_z(k).wait_recv()
            summed[span(k)] = d[span(k)].astype(F32) + e[span(k)].astype(F32)
            collected(k).start()
        loop(0, PIECES, last)
        loop(0, PIECES, lambda k: send_e(k).wait_send())

    tell.wait()
    flag[...] = mark[0] + mark[1]
    to_core.wait_send()
    for k in range(parts):
        to_chip(k).wait_send()
        forward(k).wait_send()
    for n in range(2 * STEPS):
        for k in range(3):
            exchange(n, k).wait_send()

    loop(0, PIECES, lambda k: collected(k).wait())
    trained.wait()


def second_kernel(path, d_hbm, sum_hbm, out_hbm, e, y, add, load, e_s, e_r, y_s, y_r, z_s, z_r, out_s):
    width = y.shape[0]
    o = lax.axis_index("outer")
    near = o + 1 - 2 * (o % 2)
    mid = 3 - o
    inner = jnp.logical_or(o == 1, o == 2)
    end = jnp.logical_or(o == 0, o == 3)

    barrier = pltpu.get_barrier_semaphore()
    pl.semaphore_signal(barrier, inc=1, device_id={"outer": near}, device_id_type=MESH)

    @pl.when(inner)
    def _():
        pl.semaphore_signal(barrier, inc=1, device_id={"outer": mid}, device_id_type=MESH)
        pl.semaphore_wait(barrier, 2)

    @pl.when(end)
    def _():
        pl.semaphore_wait(barrier, 1)

    def span(k):
        return span_of(width, k)

    def link(src, dst, send, recv, k, to):
        return pltpu.make_async_remote_copy(
            src_ref=src.at[span(k)], dst_ref=dst.at[span(k)], send_sem=send.at[k], recv_sem=recv.at[k],
            device_id={"outer": to}, device_id_type=MESH)

    def send_e(k):
        return link(d_hbm, e, e_s, e_r, k, near)

    def send_y(k):
        return link(e, y, y_s, y_r, k, mid)

    def send_z(k):
        return link(y, y, z_s, z_r, k, near)

    @pl.when(end)
    def _():
        loop(0, PIECES, lambda k: send_e(k).start())

    fetch = pltpu.make_async_copy(sum_hbm, add, load)
    fetch.start()
    fetch.wait()
    share = second_share(path, o)

    def written(k):
        return pltpu.make_async_copy(add.at[span(k)], out_hbm.at[span(k)], out_s.at[k])

    def take(k):
        add[span(k)] += share * y[span(k)].astype(F32)
        written(k).start()

    @pl.when(inner)
    def _():
        lag = 2

        def relay(k):
            send_e(k).wait_recv()
            send_y(k).start()

        def take_on(k):
            send_y(k).wait_recv()
            send_z(k).start()
            take(k)

        def both(k):
            relay(k)
            take_on(k - lag)
        for k in range(HEAD):
            relay(k)
            if k >= lag:
                take_on(k - lag)
        for k in range(HEAD, HEAD + lag):
            relay(k)
            take_on(k - lag)
        loop(HEAD + lag, TAIL, both)
        for k in range(TAIL, PIECES + lag):
            if k < PIECES:
                relay(k)
            take_on(k - lag)

        def settle(k):
            send_y(k).wait_send()
            send_z(k).wait_send()
        loop(0, PIECES, settle)

    @pl.when(end)
    def _():
        def last(k):
            send_z(k).wait_recv()
            take(k)
        loop(0, PIECES, last)
        loop(0, PIECES, lambda k: send_e(k).wait_send())

    loop(0, PIECES, lambda k: written(k).wait())


def finish_kernel(path, w, m, cur, summed, nw_hbm, od_hbm, nm_hbm, nw, od, nm, sems):
    o = lax.axis_index("outer")
    size = same(path, o, 0) + same(path, o, 1) + same(path, o, 2) + same(path, o, 3)
    share = 1.0 / jnp.full((1, w.shape[1]), size, F32)
    rows = w.shape[0] // 16

    def outs(k):
        r = pl.ds(pl.multiple_of(k * rows, rows), rows)
        return [pltpu.make_async_copy(x.at[r], y.at[r], sems.at[n, k])
                for n, (x, y) in enumerate(((nw, nw_hbm), (od, od_hbm), (nm, nm_hbm)))]

    def step(k, carry):
        r = pl.ds(pl.multiple_of(k * rows, rows), rows)
        outer_grad = summed[r] * share
        moment = beta_outer * m[r].astype(F32) + outer_grad
        direction = outer_grad + beta_outer * moment
        nm[r] = moment.astype(BF16)
        od[r] = ((w[r].astype(F32) - cur[r]) * (1.0 / (inner_rate * STEPS))).astype(BF16)
        nw[r] = (cur[r] - (outer_rate * inner_rate * STEPS) * direction).astype(BF16)
        for copy in outs(k):
            copy.start()
        return carry
    lax.fori_loop(0, 16, step, 0)

    def settle(k, carry):
        for copy in outs(k):
            copy.wait()
        return carry
    lax.fori_loop(0, 16, settle, 0)


ANY = pl.BlockSpec(memory_space=pl.ANY)
HBM = pl.BlockSpec(memory_space=pltpu.HBM)
SMEM = pl.BlockSpec(memory_space=pltpu.SMEM)
dma = pltpu.SemaphoreType.DMA


def phase(path, activations, cotangent, weights, earlier_delta):
    width, columns = weights.shape
    tokens = cotangent.shape[0]
    full = pltpu.VMEM((width, columns), BF16)
    wide = pltpu.VMEM((width, columns), F32)
    plane = pltpu.VMEM((tokens, columns), F32)
    line = dma((PIECES,))
    out = jax.ShapeDtypeStruct((width, columns), F32)
    return pl.pallas_call(
        phase_kernel,
        out_shape=(out, out, jax.ShapeDtypeStruct((8, 128), F32)),
        in_specs=[SMEM] + [HBM] * 4,
        out_specs=(ANY, ANY, pl.BlockSpec(memory_space=pltpu.VMEM)),
        scratch_shapes=[
            pltpu.VMEM((tokens, width), BF16), pltpu.VMEM((tokens, columns), BF16),
            full, full, full, full, full, full,
            plane, plane, plane, pltpu.VMEM((tokens, tokens), BF16),
            pltpu.VMEM((STEPS, tokens, columns), BF16), wide, wide,
            pltpu.VMEM((2 * STEPS, 8, 128), F32), pltpu.VMEM((2 * STEPS, 3, 8, 128), F32),
            pltpu.VMEM((2, 8, 128), F32),
            dma((4,)), dma((4,)), dma((4,)), dma, dma, dma((4,)), dma((4,)),
            dma((2 * STEPS, 3)), dma((2 * STEPS, 3)),
            line, line, line, line, line, line, dma((PIECES + 1,)), dma, dma,
        ],
        compiler_params=pltpu.CompilerParams(
            collective_id=1, has_side_effects=True, vmem_limit_bytes=48 * 1024 * 1024),
        cost_estimate=pl.CostEstimate(
            flops=12 * tokens * width * columns, bytes_accessed=14 * width * columns, transcendentals=0),
        name="phase",
    )(path, activations, cotangent, weights, earlier_delta)


def second(path, earlier_delta, summed):
    width, columns = summed.shape
    full = pltpu.VMEM((width, columns), BF16)
    line = dma((PIECES,))
    return pl.pallas_call(
        second_kernel,
        out_shape=jax.ShapeDtypeStruct((width, columns), F32),
        in_specs=[SMEM, ANY, ANY],
        out_specs=ANY,
        scratch_shapes=[full, full, pltpu.VMEM((width, columns), F32), dma] + [line] * 7,
        compiler_params=pltpu.CompilerParams(
            collective_id=2, has_side_effects=True, vmem_limit_bytes=32 * 1024 * 1024),
        name="second",
    )(path, earlier_delta, summed)


def finish(path, weights, momentum, cur, summed):
    width, columns = weights.shape
    out = jax.ShapeDtypeStruct((width, columns), BF16)
    return pl.pallas_call(
        finish_kernel,
        out_shape=(out, out, out),
        in_specs=[SMEM] + [pl.BlockSpec(memory_space=pltpu.VMEM)] * 4,
        out_specs=(HBM,) * 3,
        scratch_shapes=[pltpu.VMEM((width, columns), BF16)] * 3 + [dma((3, 16))],
        compiler_params=pltpu.CompilerParams(vmem_limit_bytes=32 * 1024 * 1024),
        name="finish",
    )(path, weights, momentum, cur, summed)


def line_body(activations, cotangent, weights, earlier_delta, momentum, module_path):
    delta = earlier_delta[0]
    cur, summed, flag = phase(module_path, activations[0], cotangent[0], weights[0], delta)
    outs = lax.cond(
        flag[0, 0] > 0,
        lambda t: finish(module_path, weights[0], momentum[0], cur, second(module_path, delta, t)),
        lambda t: finish(module_path, weights[0], momentum[0], cur, t),
        summed)
    return tuple(t[None] for t in outs)


def body(activations, cotangent, weights, earlier_delta, momentum, module_path):
    gathered = lax.all_gather(activations[0], "seq", axis=0, tiled=True)
    width = gathered.shape[1]
    factor = 1.0 / jnp.sqrt(jnp.float32(width))
    own_pod = lax.axis_index("outer")
    matches = module_path[:, None] == module_path[None, :]
    shared_bf = jnp.where(matches, 1.0, 0.0).astype(jnp.bfloat16)
    group_size = jnp.sum(jnp.where(matches, 1.0, 0.0).astype(jnp.float32), axis=1)
    own_size = lax.dynamic_index_in_dim(group_size, own_pod, 0, keepdims=False)
    columns = weights.shape[2]
    npods = lax.axis_size("outer")
    blocks = earlier_delta[0].reshape(npods, width // npods, columns)
    sums = jnp.einsum(
        "pq,qrc->prc",
        shared_bf,
        lax.all_to_all(blocks, "outer", split_axis=0, concat_axis=0, tiled=True),
        preferred_element_type=jnp.float32,
    )
    returned = lax.all_to_all(sums, "outer", split_axis=0, concat_axis=0, tiled=True)
    summed = returned.reshape(width, columns)
    outer_grad = summed / own_size
    moment = beta_outer * momentum[0].astype(jnp.float32) + outer_grad
    direction = outer_grad + beta_outer * moment
    sensed = cotangent[0]
    current = weights[0].astype(jnp.float32)
    for inner_step in range(STEPS):
        weight_bf = current.astype(jnp.bfloat16)
        projected = jnp.dot(gathered, weight_bf, preferred_element_type=jnp.float32) * factor
        squares = lax.psum(jnp.sum(projected * projected, axis=1), "seq")
        row_rms = jnp.sqrt(squares / width + epsilon)[:, None]
        normed = projected / row_rms
        sigmoid_y = jax.nn.sigmoid(normed)
        grad_out = sensed.astype(jnp.float32) * sigmoid_y * (1.0 + normed * (1.0 - sigmoid_y))
        products = lax.psum(jnp.sum(grad_out * normed, axis=1), "seq")
        grad_in = ((grad_out - normed * (products / width)[:, None]) / row_rms).astype(jnp.bfloat16)
        gradient = (
            lax.dot_general(
                gathered, grad_in, (((0,), (0,)), ((), ())), preferred_element_type=jnp.float32
            )
            * factor
        )
        current = current - inner_rate * gradient
    outer_delta = ((weights[0].astype(jnp.float32) - current) / (inner_rate * STEPS)).astype(
        jnp.bfloat16
    )
    new_weights = (current - outer_rate * inner_rate * STEPS * direction).astype(jnp.bfloat16)
    new_momentum = moment.astype(jnp.bfloat16)
    return (new_weights[None], outer_delta[None], new_momentum[None])


def solution(mesh):
    in_specs = (
        P(("group", "outer"), "seq", None),
        P(("group", "outer"), None, "seq"),
        P(("group", "outer"), None, "seq"),
        P(("group", "outer"), None, "seq"),
        P(("group", "outer"), None, "seq"),
        P("group"),
    )
    out_specs = (
        P(("group", "outer"), None, "seq"),
        P(("group", "outer"), None, "seq"),
        P(("group", "outer"), None, "seq"),
    )
    def run(*args):
        sizes = (mesh.shape["outer"], mesh.shape["seq"], args[0].shape[1], args[2].shape[1])
        fits = mesh.shape["group"] == 2 and sizes[:2] == (4, 4) and sizes[2] == 512 and sizes[3] % 512 == 0 and sizes[3] <= 2048
        chosen = line_body if fits else body
        return jax.shard_map(
            chosen, mesh=mesh, in_specs=in_specs, out_specs=out_specs, check_vma=False)(*args)

    return run
```
